512 devices in a mesh: along: 64 (over x, y, core), across: 8 (over z).
Axes of the slice: x: 4, y: 8, z: 8, core: 2. Of those that a mesh axis runs over, the one named last changes fastest.
Arguments:
- frames: bfloat16 [64, 3, 528, 2048], P('along', None, None, 'across'), may hold values from -6 to 6
- col_start: int32 [64, 8192], P('along', 'across'), may hold values from 0 to 252
- col_weights: bfloat16 [64, 4, 8192], P('along', None, 'across'), may hold values from 0.19921875 to 0.796875
- footprint: int32 [64, 33], P('along'), may hold values from 0 to 63, as said below
- row_start: int32 [64, 33, 8], P('along'), may hold values from 0 to 12
- row_weights: bfloat16 [64, 33, 4, 8], P('along'), may hold values from 0.19921875 to 0.796875
- seg_weight: bfloat16 [64, 33], P('along'), may hold values from 0.19921875 to 5
- feather_width: int32 [64, 8], P('along', 'across'), may hold values from 1 to 4
Outputs:
- ortho_strip: bfloat16 [3, 512, 8192], P(None, 'along', 'across')
The draws below stay inside these ranges and needn't reach their ends.
Inputs may be any that keep to these rules, and one draw needn't show every extreme that they name: footprint[f, s] = start_f + s: each frame covers 33 consecutive tiles in order, start_f never falls as f grows, start_f is 0 or f - 32 or one less, and every tile is named by some frame.
All inputs are finite; a program needn't handle non-finite values.
Results may differ from the reference program's by a relative error of at most 0.015.
Values may be sent and summed in bfloat16 or wider, within the bound.
A program may use at most 64 MiB of HBM per device.

```python
import math
import jax
import jax.numpy as jnp
from jax import lax

CH = 3
BAND = 4
TA = 8
TC = 1024
FCOLS = 256
SUBROWS = 16
SEG = 33
FRAMES = 64
FROWS = 528
FRAME_W = 2048
STRIP_W = 8192
ROWS = 512
TILES_ALONG = 64
TILES_ACROSS = 8
N_ALONG = 64
N_ACROSS = 8


def draw_footprint(key, part):
    key = jax.random.fold_in(key, 11)
    frame_ids = jnp.arange(FRAMES, dtype=jnp.int32)
    span = N_ALONG - SEG
    base = frame_ids - N_ALONG // 2
    jitter = jax.random.randint(key, (FRAMES,), -1, 1, dtype=jnp.int32)
    starts = jnp.clip(base + jitter, 0, span).astype(jnp.int32)
    starts = lax.cummax(starts, axis=0)
    starts = jnp.where(frame_ids == 0, 0, starts)
    starts = jnp.where(frame_ids == FRAMES - 1, span, starts).astype(jnp.int32)
    return (starts[:, None] + jnp.arange(SEG, dtype=jnp.int32)[None, :]).astype(jnp.int32)


def plant(drawn, rng, low, largest):
    index_at = [jax.random.randint(jax.random.fold_in(rng, axis), (), 0, length) for axis, length in enumerate(drawn.shape)]
    widest = drawn.shape.index(max(drawn.shape))
    neighbour = index_at[:widest] + [(index_at[widest] + 1) % drawn.shape[widest]] + index_at[widest + 1:]
    return drawn.at[tuple(index_at)].set(low).at[tuple(neighbour)].set(largest)


def block_scale(own_key, extent, cuts, least, top_value):
    gain = 1.0
    for position, blocks in cuts:
        heights = jax.random.uniform(jax.random.fold_in(jax.random.fold_in(own_key, 6), position), (blocks,), jnp.float32, least / len(cuts), top_value / len(cuts))
        gain = gain * jnp.repeat(jnp.exp(heights), extent[position] // blocks).reshape((-1,) + (1,) * (len(extent) - 1 - position))
    return gain


def bell_draw(key, shape, width, reach, cuts=(), kind=jnp.bfloat16):
    gain = block_scale(key, shape, cuts, -0.22, 0.18) if cuts else 1.0
    values = jax.random.normal(key, shape, jnp.float32) * width * gain
    return jnp.minimum(jnp.maximum(values, -reach), reach).astype(kind)


def setup_inputs(seed: int = 0) -> dict:
    key_list = jax.random.split(jax.random.key(seed), 9)
    frames = bell_draw(key_list[0], (FRAMES, CH, FROWS, FRAME_W), 1.0, 6.0, ((0, 64), (3, 8)))
    col_start = plant(jax.random.randint(key_list[1], (FRAMES, STRIP_W), 0, FCOLS - BAND + 1), jax.random.fold_in(key_list[1], 1), 0, FCOLS - BAND).astype(jnp.int32)
    col_weights = jnp.clip(0.19921875 + 0.59765625 * jax.random.uniform(key_list[2], (FRAMES, BAND, STRIP_W), jnp.float32) ** block_scale(key_list[2], (FRAMES, BAND, STRIP_W), ((0, 64), (2, 8)), -0.2, 0.2), 0.19921875, 0.796875).astype(jnp.bfloat16)
    footprint = draw_footprint(jax.random.fold_in(key_list[8], 71), 0)
    row_start = plant(jax.random.randint(key_list[4], (FRAMES, SEG, TA), 0, SUBROWS - BAND + 1), jax.random.fold_in(key_list[4], 1), 0, SUBROWS - BAND).astype(jnp.int32)
    row_weights = jnp.clip(0.19921875 + 0.59765625 * jax.random.uniform(key_list[5], (FRAMES, SEG, BAND, TA), jnp.float32) ** block_scale(key_list[5], (FRAMES, SEG, BAND, TA), ((0, 64),), -0.2, 0.2), 0.19921875, 0.796875).astype(jnp.bfloat16)
    seg_weight = jnp.clip(jnp.exp(math.log(5.0) - 3.2227897 * jax.random.uniform(key_list[6], (FRAMES, SEG), jnp.float32) ** block_scale(key_list[6], (FRAMES, SEG), ((0, 64),), -0.2, 0.2)), 0.19921875, 5.0).astype(jnp.bfloat16)
    feather_width = plant(jax.random.randint(key_list[7], (TILES_ALONG, TILES_ACROSS), 1, TA // 2 + 1), jax.random.fold_in(key_list[7], 1), 1, (TA // 2 + 1) - 1).astype(jnp.int32)
    return {"frames": frames, "col_start": col_start, "col_weights": col_weights, "footprint": footprint, "row_start": row_start, "row_weights": row_weights, "seg_weight": seg_weight, "feather_width": feather_width}


def band_matrix(starts, weights, length):
    positions = jnp.arange(length, dtype=jnp.int32)
    offsets = positions - starts[..., None]
    result = jnp.zeros(offsets.shape, jnp.float32)
    for step in range(BAND):
        result = result + jnp.where(offsets == step, weights[..., step, :, None].astype(jnp.float32), jnp.float32(0.0))
    return result


def reference(frames, col_start, col_weights, footprint, row_start, row_weights, seg_weight, feather_width):
    shard_of = (jnp.arange(STRIP_W, dtype=jnp.int32) // TC).astype(jnp.int32)
    band_pos = jnp.arange(BAND, dtype=jnp.int32)

    def per_frame(carry, inputs):
        numerator, denominator = carry
        image, starts, weights, tiles, rstarts, rweights, blend = inputs
        columns = (shard_of * FCOLS + starts)[None, :] + band_pos[:, None]
        picked = image[:, :, columns].astype(jnp.float32)
        col_part = jnp.sum(picked * weights.astype(jnp.float32)[None, None], axis=2).astype(jnp.bfloat16)
        segments = col_part.reshape(CH, SEG, SUBROWS, STRIP_W).astype(jnp.float32)
        rows_matrix = band_matrix(rstarts, rweights, SUBROWS)
        pieces = jnp.einsum("sik,cskw->sciw", rows_matrix, segments, precision=lax.Precision.HIGHEST).astype(jnp.bfloat16)
        scaled = blend.astype(jnp.float32)[:, None, None, None] * pieces.astype(jnp.float32)
        numerator = numerator.at[tiles].add(scaled)
        denominator = denominator.at[tiles].add(blend.astype(jnp.float32))
        return (numerator, denominator), None

    start_num = jnp.zeros((N_ALONG, CH, TA, STRIP_W), jnp.float32)
    start_den = jnp.zeros((N_ALONG,), jnp.float32)
    (numerator, denominator), _ = lax.scan(per_frame, (start_num, start_den), (frames, col_start, col_weights, footprint, row_start, row_weights, seg_weight))
    blended = (numerator / denominator[:, None, None, None]).astype(jnp.bfloat16)
    values = blended.astype(jnp.float32)

    widths = feather_width.astype(jnp.float32)
    wide_cols = jnp.repeat(widths, TC, axis=1)
    row_pos = jnp.arange(TA, dtype=jnp.float32)
    ramp_top = jnp.maximum(0.0, 1.0 - row_pos[None, :, None] / wide_cols[:, None, :])
    ramp_bottom = jnp.maximum(0.0, 1.0 - (TA - 1 - row_pos)[None, :, None] / wide_cols[:, None, :])
    tile_ids = jnp.arange(N_ALONG)
    has_up = (tile_ids > 0).astype(jnp.float32)
    has_down = (tile_ids < N_ALONG - 1).astype(jnp.float32)
    blank_row = jnp.zeros((1, CH, STRIP_W), jnp.float32)
    above = jnp.concatenate([blank_row, values[:-1, :, TA - 1, :]], axis=0)
    below = jnp.concatenate([values[1:, :, 0, :], blank_row], axis=0)
    diff_up = has_up[:, None, None] * (above - values[:, :, 0, :])
    diff_down = has_down[:, None, None] * (below - values[:, :, TA - 1, :])
    result = values + 0.5 * ramp_top[:, None] * diff_up[:, :, None, :]
    result = result + 0.5 * ramp_bottom[:, None] * diff_down[:, :, None, :]

    by_cols = values.reshape(N_ALONG, CH, TA, N_ACROSS, TC)
    col_pos = jnp.arange(TC, dtype=jnp.float32)
    ramp_left = jnp.maximum(0.0, 1.0 - col_pos[None, None, :] / widths[:, :, None])
    ramp_right = jnp.maximum(0.0, 1.0 - (TC - 1 - col_pos)[None, None, :] / widths[:, :, None])
    across_ids = jnp.arange(N_ACROSS)
    has_left = (across_ids > 0).astype(jnp.float32)
    has_right = (across_ids < N_ACROSS - 1).astype(jnp.float32)
    blank_col = jnp.zeros((N_ALONG, CH, TA, 1), jnp.float32)
    left = jnp.concatenate([blank_col, by_cols[:, :, :, :-1, TC - 1]], axis=3)
    right = jnp.concatenate([by_cols[:, :, :, 1:, 0], blank_col], axis=3)
    diff_left = has_left * (left - by_cols[:, :, :, :, 0])
    diff_right = has_right * (right - by_cols[:, :, :, :, TC - 1])
    side = 0.5 * ramp_left[:, None, None] * diff_left[..., None] + 0.5 * ramp_right[:, None, None] * diff_right[..., None]
    result = result + side.reshape(N_ALONG, CH, TA, STRIP_W)
    ortho_strip = jnp.transpose(result, (1, 0, 2, 3)).reshape(CH, ROWS, STRIP_W)
    return ortho_strip.astype(jnp.bfloat16)
```

```python
import functools

import jax
import jax.numpy as jnp
from jax import lax
from jax.experimental import pallas as pl
from jax.experimental.pallas import tpu as pltpu
from jax.sharding import PartitionSpec as P

MESH = pl.DeviceIdType.MESH
F32 = jnp.float32
BF16 = jnp.bfloat16
NX, NY, NC = 4, 8, 2
PEERS = NX * NC
CHUNKS = ((4, 3), (5, 2), (6, 1), (7, 0))


def taps(delta, weights):
    value = jnp.zeros(delta.shape, F32)
    for step, weight in enumerate(weights):
        value = jnp.where(delta == float(step), weight, value)
    return value


def kernel(
    nz, frames, table, places, own_params, width_ref, out,
    image, lmat, outbox, inbox, params, cmat, ysend, yrecv, dsend, drecv, hsend, hrecv, ssend, srecv,
    load_sem, px_s, px_r, x_s, x_r, y_s, y_r, d_s, d_r, h_s, h_r,
):
    a = lax.axis_index("along")
    z = lax.axis_index("across")
    x, y, c = a // (NY * NC), (a // NC) % NY, a % NC

    def along(xx, yy, cc):
        return ((xx % NX) * NY + (yy % NY)) * NC + cc

    def x_peer(r):
        return (along(x + r % NX, y, (c + r // NX) % NC), z)

    def y_peer(rel):
        return (along(x, y + rel, c), z)

    after, before = (a + 1) % 64, (a + 63) % 64
    extra = (a + 63 + 2 * c) % 64
    barrier = pltpu.get_barrier_semaphore()
    friends = [x_peer(r) for r in range(1, PEERS)] + [y_peer(r) for r in range(1, NY)] + [(extra, z)]
    if nz > 1:
        friends += [(a, (z + 1) % nz), (a, (z + nz - 1) % nz)]
    for friend in friends:
        pl.semaphore_signal(barrier, inc=1, device_id=friend, device_id_type=MESH)

    load = pltpu.make_async_copy(frames.at[0], image.at[:, pl.ds(0, 528), :], load_sem)
    load.start()
    image[:, 528:, :] = jnp.zeros((3, 112, 256), BF16)

    row = lax.broadcasted_iota(jnp.int32, (128, 128), 0)
    lane = lax.broadcasted_iota(jnp.int32, (128, 128), 1)
    spread_row = lax.broadcasted_iota(jnp.int32, (128, 768), 0)
    spread_lane = lax.broadcasted_iota(jnp.int32, (128, 768), 1)
    spread = (spread_row // 8 == spread_lane // 128).astype(F32).astype(BF16)
    same = ((lane % 8) == (row % 8)).astype(F32)
    peer = row // 16
    group = (x + peer % NX) % NX
    core = (c + peer // NX) % NC
    first = (row // 8) % 2 == 0
    fp_row = places[0:1, :]
    start = places[0:1, 0:1]
    position = lax.broadcasted_iota(jnp.int32, (256, 128), 0).astype(F32)

    def make_matrix(r):
        def slab(n, carry):
            for half in range(2):
                j = n * 2 + half
                rows = [params[r, pl.ds(b * 8 + j, 1), :].astype(F32) for b in range(5)]
                value = taps(position - rows[4], rows[:4])
                cmat[n, r * 256:(r + 1) * 256, half * 128:(half + 1) * 128] = value.astype(BF16)
            return carry

        for n in range(4):
            slab(n, 0)

    def make_chunk(k):
        rel = jnp.where(first, CHUNKS[k][0], CHUNKS[k][1])
        tile = group * 16 + 2 * ((y + rel) % NY) + core
        hit = (tile == fp_row).astype(F32).astype(BF16)
        picked = jnp.dot(hit, table[...], preferred_element_type=F32) * same
        wide = jnp.dot(picked.astype(BF16), spread, preferred_element_type=F32)
        base = (lane - 16 * (tile - start)).astype(F32) - wide[:, :128]
        weights = [wide[:, 128 * (b + 1):128 * (b + 2)] for b in range(4)]
        for part in range(5):
            lmat[:, part * 128:(part + 1) * 128] = taps(base + float(128 * part), weights).astype(BF16)
        blend = jnp.concatenate([wide[:, 640:], wide[:, 640:]], axis=1)
        rows = [jnp.dot(lmat[...], image[ch], preferred_element_type=F32) * blend for ch in range(3)]
        for r in range(PEERS):
            block = jnp.concatenate(
                [rows[ch][r * 16 + m * 8:r * 16 + m * 8 + 8] for m in range(2) for ch in range(3)], axis=0
            ).astype(BF16)
            if r == 0:
                inbox[k, :, 0:256] = block
            else:
                outbox[k, r] = block

    def copy_params(r):
        return pltpu.make_async_remote_copy(
            src_ref=params.at[0], dst_ref=params.at[r], send_sem=px_s.at[r], recv_sem=px_r.at[r],
            device_id=x_peer(r), device_id_type=MESH,
        )

    def copy_chunk(k, r):
        return pltpu.make_async_remote_copy(
            src_ref=outbox.at[k, r], dst_ref=inbox.at[k, :, pl.ds(r * 256, 256)],
            send_sem=x_s.at[k, r], recv_sem=x_r.at[k, r], device_id=x_peer(r), device_id_type=MESH,
        )

    def copy_sum(rel):
        return pltpu.make_async_remote_copy(
            src_ref=ysend.at[rel], dst_ref=yrecv.at[rel], send_sem=y_s.at[rel], recv_sem=y_r.at[rel],
            device_id=y_peer(rel), device_id_type=MESH,
        )

    def copy_weight(rel):
        return pltpu.make_async_remote_copy(
            src_ref=dsend, dst_ref=drecv.at[rel], send_sem=d_s.at[rel], recv_sem=d_r.at[rel],
            device_id=y_peer(rel), device_id_type=MESH,
        )

    order = (2, 6, 1, 3, 5, 7, 4)
    params[0] = own_params[...]
    load.wait()
    make_chunk(0)
    pl.semaphore_wait(barrier, len(friends))
    for r in order:
        copy_params(r).start()
    for r in order:
        copy_chunk(0, r).start()
    for k in range(1, 4):
        make_chunk(k)
        for r in order:
            copy_chunk(k, r).start()
    make_matrix(0)
    weight = params[0, 32:48, :].astype(F32)
    for r in (4, 1, 3, 5, 7, 2, 6):
        copy_params(r).wait_recv()
        make_matrix(r)
        weight = weight + params[r, 32:48, :].astype(F32)
    weight = weight[8:16]
    dsend[...] = weight
    for rel in range(1, NY):
        copy_weight(rel).start()

    own = None
    for k in range(4):
        for r in range(1, PEERS):
            copy_chunk(k, r).wait_recv()
        left = inbox[k]
        total = jnp.concatenate(
            [jnp.dot(left, cmat[n], preferred_element_type=F32) for n in range(4)], axis=1
        )
        for m in range(2):
            rel = CHUNKS[k][m]
            part = total[m * 24:(m + 1) * 24]
            folded = jnp.concatenate([part[:, :512], part[:, 512:]], axis=0)
            if rel == 0:
                own = folded
            else:
                ysend[rel] = folded.astype(BF16)
                copy_sum(rel).start()

    for rel in range(1, NY):
        copy_weight(rel).wait_recv()
        weight = weight + drecv[rel]
    here = lax.broadcasted_iota(jnp.int32, (8, 128), 1) == a
    divisor = jnp.sum(jnp.where(here, weight, 0.0), axis=1, keepdims=True)[0:1]
    for rel in (4, 3, 5, 2, 6, 1, 7):
        copy_sum(rel).wait_recv()
        own = own + yrecv[rel].astype(F32)
    own = own / divisor
    values = jnp.concatenate([own[:24], own[24:]], axis=1).astype(BF16).astype(F32)

    blank = jnp.zeros((1, 256), F32)

    def edge_rows(i):
        pieces = []
        for j in range(4):
            pieces += [values[ch * 8 + i:ch * 8 + i + 1, j * 256:(j + 1) * 256] for ch in range(3)] + [blank]
        return jnp.concatenate(pieces, axis=0).astype(BF16)

    pad = jnp.zeros((8, 128), F32)
    hsend[0] = edge_rows(7)
    hsend[1] = edge_rows(0)
    ssend[0] = jnp.concatenate([values[:, 896:], pad], axis=0).astype(BF16)
    ssend[1] = jnp.concatenate([values[:, :128], pad], axis=0).astype(BF16)
    halo = [
        pltpu.make_async_remote_copy(
            src_ref=hsend.at[side], dst_ref=hrecv.at[side], send_sem=h_s.at[side], recv_sem=h_r.at[side],
            device_id=(after if side == 0 else before, z), device_id_type=MESH,
        )
        for side in range(2)
    ]
    if nz > 1:
        halo += [
            pltpu.make_async_remote_copy(
                src_ref=ssend.at[side], dst_ref=srecv.at[side], send_sem=h_s.at[2 + side],
                recv_sem=h_r.at[2 + side],
                device_id=(a, (z + 1) % nz if side == 0 else (z + nz - 1) % nz), device_id_type=MESH,
            )
            for side in range(2)
        ]
    for copy in halo:
        copy.start()
    for copy in halo:
        copy.wait_recv()

    def opened(side):
        got = hrecv[side].astype(F32)
        return [
            jnp.concatenate([got[4 * j + ch:4 * j + ch + 1] for j in range(4)], axis=1) for ch in range(3)
        ]

    width = width_ref[...].astype(F32)
    row8 = lax.broadcasted_iota(jnp.int32, (8, 1024), 0).astype(F32)
    col8 = lax.broadcasted_iota(jnp.int32, (8, 1024), 1).astype(F32)
    has_up = (a > 0).astype(F32)
    has_down = (a < 63).astype(F32)
    has_left = (z > 0).astype(F32)
    has_right = (z < nz - 1).astype(F32)
    top = 0.5 * jnp.maximum(0.0, 1.0 - row8 / width) * has_up
    bottom = 0.5 * jnp.maximum(0.0, 1.0 - (7.0 - row8) / width) * has_down
    ramp_left = 0.5 * jnp.maximum(0.0, 1.0 - col8 / width) * has_left
    ramp_right = 0.5 * jnp.maximum(0.0, 1.0 - (1023.0 - col8) / width) * has_right
    up, down = opened(0), opened(1)
    for ch in range(3):
        tile = values[ch * 8:(ch + 1) * 8]
        result = tile + top * (up[ch] - tile[0:1]) + bottom * (down[ch] - tile[7:8])
        if nz > 1:
            left_col = srecv[0, ch * 8:(ch + 1) * 8, 127:128].astype(F32)
            right_col = srecv[1, ch * 8:(ch + 1) * 8, 0:1].astype(F32)
            result = result + ramp_left * (left_col - tile[:, 0:1]) + ramp_right * (right_col - tile[:, 1023:])
        out[ch] = result.astype(BF16)

    for r in range(1, PEERS):
        copy_params(r).wait_send()
        for k in range(4):
            copy_chunk(k, r).wait_send()
    for rel in range(1, NY):
        copy_weight(rel).wait_send()
        copy_sum(rel).wait_send()
    for copy in halo:
        copy.wait_send()


def body(
    frames, col_start, col_weights, footprint, row_start, row_weights, seg_weight, feather_width
):
    nz = lax.axis_size("across")
    blend = jnp.broadcast_to(seg_weight[0][:, None], (33, 8))
    table = jnp.concatenate(
        [row_start[0].astype(BF16), row_weights[0].reshape(33, 32), blend], axis=1
    )
    table = jnp.pad(table, ((0, 95), (0, 80)))
    places = jnp.broadcast_to(jnp.pad(footprint, ((0, 0), (0, 95)), constant_values=-1), (8, 128))
    tiles = jnp.arange(128, dtype=jnp.int32)
    by_tile = jnp.sum(
        jnp.where(footprint[0][:, None] == tiles[None, :], seg_weight[0].astype(F32)[:, None], 0.0), axis=0
    ).astype(BF16)
    own_params = jnp.concatenate(
        [
            col_weights[0].reshape(32, 128),
            col_start[0].astype(BF16).reshape(8, 128),
            jnp.broadcast_to(by_tile[None, :], (8, 128)),
        ],
        axis=0,
    )
    vmem = pl.BlockSpec(memory_space=pltpu.VMEM)
    dma = pltpu.SemaphoreType.DMA
    return pl.pallas_call(
        functools.partial(kernel, nz),
        out_shape=jax.ShapeDtypeStruct((3, 8, 1024), BF16),
        in_specs=[pl.BlockSpec(memory_space=pl.ANY), vmem, vmem, vmem, vmem],
        out_specs=vmem,
        scratch_shapes=[
            pltpu.VMEM((3, 640, 256), BF16),
            pltpu.VMEM((128, 640), BF16),
            pltpu.VMEM((4, PEERS, 48, 256), BF16),
            pltpu.VMEM((4, 48, 256 * PEERS), BF16),
            pltpu.VMEM((PEERS, 48, 128), BF16),
            pltpu.VMEM((4, 256 * PEERS, 256), BF16),
            pltpu.VMEM((NY, 48, 512), BF16),
            pltpu.VMEM((NY, 48, 512), BF16),
            pltpu.VMEM((8, 128), F32),
            pltpu.VMEM((NY, 8, 128), F32),
            pltpu.VMEM((2, 16, 256), BF16),
            pltpu.VMEM((2, 16, 256), BF16),
            pltpu.VMEM((2, 32, 128), BF16),
            pltpu.VMEM((2, 32, 128), BF16),
            dma,
            dma((PEERS,)),
            dma((PEERS,)),
            dma((4, PEERS)),
            dma((4, PEERS)),
            dma((NY,)),
            dma((NY,)),
            dma((NY,)),
            dma((NY,)),
            dma((4,)),
            dma((4,)),
        ],
        compiler_params=pltpu.CompilerParams(
            collective_id=0, has_side_effects=True, vmem_limit_bytes=32 * 2**20
        ),
    )(frames, table, places, own_params, feather_width)


def solution(mesh):
    placed = (
        P("along", None, None, "across"),
        P("along", "across"),
        P("along", None, "across"),
        P("along", None),
        P("along", None, None),
        P("along", None, None, None),
        P("along", None),
        P("along", "across"),
    )
    return jax.shard_map(
        body, mesh=mesh, in_specs=placed, out_specs=P(None, "along", "across"), check_vma=False
    )
```

```python
import functools

import jax
import jax.numpy as jnp
from jax import lax
from jax.experimental import pallas as pl
from jax.experimental.pallas import tpu as pltpu
from jax.sharding import PartitionSpec as P

MESH = pl.DeviceIdType.MESH
F32 = jnp.float32
BF16 = jnp.bfloat16
NX, NY, NC = 4, 8, 2
PEERS = NX * NC
CHUNKS = ((4, 3), (5, 2), (6, 1), (7, 0))
GROUPS = ((0, 4), (1, 5), (3, 7), (2, 6))
PLACE = {r: 2 * g + i for g, group in enumerate(GROUPS) for i, r in enumerate(group)}


def taps(delta, weights):
    value = jnp.zeros(delta.shape, delta.dtype)
    for step, weight in enumerate(weights):
        value = jnp.where(delta == jnp.asarray(step, delta.dtype), weight, value)
    return value


def kernel(
    nz, frames, col_start, col_weights, footprint, row_start, row_weights, seg_weight, feather, out,
    image, starts_in, taps_in, places_in, rstart_in, rtaps_in, blend_in, width_in,
    table, places, blends, gather, lmat, outbox, inbox, params, cmat, ysend, yrecv, dsend, drecv, hsend, hrecv, ssend, srecv,
    load_sem, small_sem, px_s, px_r, x_s, x_r, y_s, y_r, d_s, d_r, h_s, h_r,
):
    a = lax.axis_index("along")
    z = lax.axis_index("across")
    x, y, c = a // (NY * NC), (a // NC) % NY, a % NC

    def along(xx, yy, cc):
        return ((xx % NX) * NY + (yy % NY)) * NC + cc

    def x_peer(r):
        return (along(x + r % NX, y, (c + r // NX) % NC), z)

    def y_peer(rel):
        return (along(x, y + rel, c), z)

    after, before = (a + 1) % 64, (a + 63) % 64
    extra = (a + 63 + 2 * c) % 64
    barrier = pltpu.get_barrier_semaphore()
    friends = [x_peer(r) for r in range(1, PEERS)] + [y_peer(r) for r in range(1, NY)] + [(extra, z)]
    if nz > 1:
        friends += [(a, (z + 1) % nz), (a, (z + nz - 1) % nz)]
    for friend in friends:
        pl.semaphore_signal(barrier, inc=1, device_id=friend, device_id_type=MESH)

    load = pltpu.make_async_copy(frames.at[0], image.at[:, pl.ds(0, 528), :], load_sem)
    load.start()
    small = [
        pltpu.make_async_copy(src, dst, small_sem.at[i])
        for i, (src, dst) in enumerate(
            (
                (footprint, places_in),
                (row_start.at[0], rstart_in),
                (row_weights.at[0], rtaps_in),
                (seg_weight, blend_in),
                (col_weights.at[0], taps_in),
                (col_start, starts_in),
                (feather, width_in),
            )
        )
    ]
    for copy in small:
        copy.start()
    image[:, 528:, :] = jnp.zeros((3, 112, 256), BF16)
    places[...] = jnp.full((8, 128), -1, jnp.int32)
    blends[...] = jnp.zeros((8, 128), F32)
    for copy in small:
        copy.wait()
    places[0:1, 0:33] = places_in[...]
    blends[0:1, 0:33] = blend_in[...].astype(F32)
    table[...] = jnp.zeros((128, 128), F32)
    table[0:8, 0:33] = rstart_in[...].astype(F32)
    for b in range(4):
        table[8 * (b + 1):8 * (b + 2), 0:33] = rtaps_in[b].astype(F32)

    row = lax.broadcasted_iota(jnp.int32, (128, 128), 0)
    lane = lax.broadcasted_iota(jnp.int32, (128, 128), 1)
    spread_row = lax.broadcasted_iota(jnp.int32, (128, 640), 0)
    spread_lane = lax.broadcasted_iota(jnp.int32, (128, 640), 1)
    spread = (spread_row // 8 == spread_lane // 128).astype(F32).astype(BF16)
    same = ((lane % 8) == (row % 8)).astype(F32)
    peer = row // 16
    group = (x + peer % NX) % NX
    core = (c + peer // NX) % NC
    first = (row // 8) % 2 == 0
    fp_row = places[0:1, :]
    start = places[0:1, 0:1]
    blend_row = blends[0:1, :]
    ones = jnp.ones((128, 128), BF16)
    rows_table = table[...].astype(BF16)
    by_tile = jnp.dot(
        blends[...].astype(BF16), (lane - start == row).astype(F32).astype(BF16), preferred_element_type=F32
    )
    col_taps = taps_in[...].astype(F32)
    col_first = starts_in[...].astype(F32)
    for j in range(8):
        for b in range(4):
            gather[b * 8 + j:b * 8 + j + 1, :] = col_taps[b:b + 1, j * 128:(j + 1) * 128]
        gather[32 + j:33 + j, :] = col_first[:, j * 128:(j + 1) * 128]
    gather[40:48, :] = by_tile
    position = lax.broadcasted_iota(jnp.int32, (256, 128), 0).astype(F32).astype(BF16)

    def make_matrix(r):
        for j in range(8):
            rows = [params[r, b * 8 + j:b * 8 + j + 1, :] for b in range(5)]
            value = taps(position - rows[4], rows[:4])
            cmat[j // 2, PLACE[r] * 256:(PLACE[r] + 1) * 256, (j % 2) * 128:(j % 2 + 1) * 128] = value

    def make_chunk(k):
        rel = jnp.where(first, CHUNKS[k][0], CHUNKS[k][1])
        tile = group * 16 + 2 * ((y + rel) % NY) + core
        hit = (tile == fp_row).astype(F32)
        picked = same * lax.dot_general(
            hit.astype(BF16), rows_table, (((1,), (1,)), ((), ())), preferred_element_type=F32
        )
        blend = jnp.dot((hit * blend_row).astype(BF16), ones, preferred_element_type=F32)
        wide = jnp.dot(picked.astype(BF16), spread, preferred_element_type=F32)
        base = (lane - 16 * (tile - start)).astype(F32) - wide[:, :128]
        weights = [wide[:, 128 * (b + 1):128 * (b + 2)] for b in range(4)]
        for part in range(5):
            lmat[:, part * 128:(part + 1) * 128] = taps(base + float(128 * part), weights).astype(BF16)
        blend = jnp.concatenate([blend, blend], axis=1)
        rows = [jnp.dot(lmat[...], image[ch], preferred_element_type=F32) * blend for ch in range(3)]
        for r in range(PEERS):
            block = jnp.concatenate(
                [rows[ch][r * 16 + m * 8:r * 16 + m * 8 + 8] for m in range(2) for ch in range(3)], axis=0
            ).astype(BF16)
            if r == 0:
                inbox[k, :, 0:256] = block
            else:
                outbox[k, r] = block

    def copy_params(r):
        return pltpu.make_async_remote_copy(
            src_ref=params.at[max(r - NX, 0)], dst_ref=params.at[r], send_sem=px_s.at[r], recv_sem=px_r.at[r],
            device_id=x_peer(min(r, NX)), device_id_type=MESH,
        )

    def copy_chunk(k, r):
        return pltpu.make_async_remote_copy(
            src_ref=outbox.at[k, r], dst_ref=inbox.at[k, :, pl.ds(PLACE[r] * 256, 256)],
            send_sem=x_s.at[k, r], recv_sem=x_r.at[k, r], device_id=x_peer(r), device_id_type=MESH,
        )

    def copy_sum(slot):
        hop = {0: 6, 1: 1, 2: 2, 3: 1, 4: 2, 5: 7, 6: 6, 7: 7}[slot]
        lanes = {0: pl.ds(256, 256), 4: pl.ds(0, 256)}.get(slot, pl.ds(0, 512))
        return pltpu.make_async_remote_copy(
            src_ref=ysend.at[slot or 4, :, lanes], dst_ref=yrecv.at[slot, :, lanes],
            send_sem=y_s.at[slot], recv_sem=y_r.at[slot], device_id=y_peer(hop), device_id_type=MESH,
        )

    def copy_weight(rel):
        return pltpu.make_async_remote_copy(
            src_ref=dsend, dst_ref=drecv.at[rel], send_sem=d_s.at[rel], recv_sem=d_r.at[rel],
            device_id=y_peer(rel), device_id_type=MESH,
        )

    order = (2, 6, 1, 3, 5, 7, 4)
    params[0] = gather[...].astype(BF16)
    load.wait()
    make_chunk(0)
    pl.semaphore_wait(barrier, len(friends))
    for r in (2, 1, 3, 4):
        copy_params(r).start()
    for r in order:
        copy_chunk(0, r).start()
    make_chunk(1)
    for r in order:
        copy_chunk(1, r).start()
    make_chunk(2)
    for r in order:
        copy_chunk(2, r).start()
    make_chunk(3)
    for r in order:
        copy_chunk(3, r).start()
    make_matrix(0)
    weight = params[0, 32:48, :].astype(F32)
    for r in (4, 1, 3, 2, 5, 7, 6):
        copy_params(r).wait_recv()
        if r < NX:
            copy_params(r + NX).start()
        make_matrix(r)
        weight = weight + params[r, 32:48, :].astype(F32)
    weight = weight[8:16]
    dsend[...] = weight
    for rel in range(1, NY):
        copy_weight(rel).start()

    held = {}
    for k in range(4):
        total = [0.0] * 4
        for g, group in enumerate(GROUPS):
            for r in group:
                if r:
                    copy_chunk(k, r).wait_recv()
            left = inbox[k, :, g * 512:(g + 1) * 512]
            total = [
                total[n] + jnp.dot(left, cmat[n, g * 512:(g + 1) * 512], preferred_element_type=F32)
                for n in range(4)
            ]
        total = jnp.concatenate(total, axis=1)
        for m in range(2):
            rel = CHUNKS[k][m]
            part = total[m * 24:(m + 1) * 24]
            held[rel] = folded = jnp.concatenate([part[:, :512], part[:, 512:]], axis=0)
            if rel in (1, 3, 4, 5, 7):
                ysend[rel] = folded.astype(BF16)
                copy_sum(rel).start()
            if rel == 4:
                copy_sum(0).start()
        if k == 2:
            for rel, near, far, lanes in ((2, 3, 4, 0), (6, 5, 0, 256)):
                copy_sum(near).wait_recv()
                copy_sum(far).wait_recv()
                half = yrecv[far, :, lanes:lanes + 256].astype(F32)
                blank = jnp.zeros((48, 256), F32)
                half = jnp.concatenate([blank, half] if lanes else [half, blank], axis=1)
                ysend[rel] = (held[rel] + yrecv[near].astype(F32) + half).astype(BF16)
                copy_sum(rel).start()
    own = held[0]

    for rel in range(1, NY):
        copy_weight(rel).wait_recv()
        weight = weight + drecv[rel]
    here = lax.broadcasted_iota(jnp.int32, (8, 128), 1) == a
    divisor = jnp.sum(jnp.where(here, weight, 0.0), axis=1, keepdims=True)[0:1]
    for rel in (2, 6, 1, 7):
        copy_sum(rel).wait_recv()
        own = own + yrecv[rel].astype(F32)
    own = own / divisor
    values = jnp.concatenate([own[:24], own[24:]], axis=1).astype(BF16).astype(F32)

    blank = jnp.zeros((1, 256), F32)

    def edge_rows(i):
        pieces = []
        for j in range(4):
            pieces += [values[ch * 8 + i:ch * 8 + i + 1, j * 256:(j + 1) * 256] for ch in range(3)] + [blank]
        return jnp.concatenate(pieces, axis=0).astype(BF16)

    pad = jnp.zeros((8, 128), F32)
    hsend[0] = edge_rows(7)
    hsend[1] = edge_rows(0)
    ssend[0] = jnp.concatenate([values[:, 896:], pad], axis=0).astype(BF16)
    ssend[1] = jnp.concatenate([values[:, :128], pad], axis=0).astype(BF16)
    halo = [
        pltpu.make_async_remote_copy(
            src_ref=hsend.at[side], dst_ref=hrecv.at[side], send_sem=h_s.at[side], recv_sem=h_r.at[side],
            device_id=(after if side == 0 else before, z), device_id_type=MESH,
        )
        for side in range(2)
    ]
    if nz > 1:
        halo += [
            pltpu.make_async_remote_copy(
                src_ref=ssend.at[side], dst_ref=srecv.at[side], send_sem=h_s.at[2 + side],
                recv_sem=h_r.at[2 + side],
                device_id=(a, (z + 1) % nz if side == 0 else (z + nz - 1) % nz), device_id_type=MESH,
            )
            for side in range(2)
        ]
    for copy in halo:
        copy.start()
    for copy in halo:
        copy.wait_recv()

    def opened(side):
        got = hrecv[side].astype(F32)
        return [
            jnp.concatenate([got[4 * j + ch:4 * j + ch + 1] for j in range(4)], axis=1) for ch in range(3)
        ]

    width = width_in[...].astype(F32)
    row8 = lax.broadcasted_iota(jnp.int32, (8, 1024), 0).astype(F32)
    col8 = lax.broadcasted_iota(jnp.int32, (8, 1024), 1).astype(F32)
    has_up = (a > 0).astype(F32)
    has_down = (a < 63).astype(F32)
    has_left = (z > 0).astype(F32)
    has_right = (z < nz - 1).astype(F32)
    top = 0.5 * jnp.maximum(0.0, 1.0 - row8 / width) * has_up
    bottom = 0.5 * jnp.maximum(0.0, 1.0 - (7.0 - row8) / width) * has_down
    ramp_left = 0.5 * jnp.maximum(0.0, 1.0 - col8 / width) * has_left
    ramp_right = 0.5 * jnp.maximum(0.0, 1.0 - (1023.0 - col8) / width) * has_right
    up, down = opened(0), opened(1)
    for ch in range(3):
        tile = values[ch * 8:(ch + 1) * 8]
        result = tile + top * (up[ch] - tile[0:1]) + bottom * (down[ch] - tile[7:8])
        if nz > 1:
            left_col = srecv[0, ch * 8:(ch + 1) * 8, 127:128].astype(F32)
            right_col = srecv[1, ch * 8:(ch + 1) * 8, 0:1].astype(F32)
            result = result + ramp_left * (left_col - tile[:, 0:1]) + ramp_right * (right_col - tile[:, 1023:])
        out[ch] = result.astype(BF16)

    for r in range(1, PEERS):
        copy_params(r).wait_send()
        for k in range(4):
            copy_chunk(k, r).wait_send()
    for rel in range(1, NY):
        copy_weight(rel).wait_send()
    for slot in range(NY):
        copy_sum(slot).wait_send()
    for copy in halo:
        copy.wait_send()


def body(
    frames, col_start, col_weights, footprint, row_start, row_weights, seg_weight, feather_width
):
    nz = lax.axis_size("across")
    vmem = pl.BlockSpec(memory_space=pltpu.VMEM)
    dma = pltpu.SemaphoreType.DMA
    return pl.pallas_call(
        functools.partial(kernel, nz),
        out_shape=jax.ShapeDtypeStruct((3, 8, 1024), BF16),
        in_specs=[pl.BlockSpec(memory_space=pltpu.HBM)] * 8,
        out_specs=vmem,
        scratch_shapes=[
            pltpu.VMEM((3, 640, 256), BF16),
            pltpu.VMEM((1, 1024), jnp.int32),
            pltpu.VMEM((4, 1024), BF16),
            pltpu.VMEM((1, 33), jnp.int32),
            pltpu.VMEM((8, 33), jnp.int32),
            pltpu.VMEM((4, 8, 33), BF16),
            pltpu.VMEM((1, 33), BF16),
            pltpu.VMEM((1, 1), jnp.int32),
            pltpu.VMEM((128, 128), F32),
            pltpu.VMEM((8, 128), jnp.int32),
            pltpu.VMEM((8, 128), F32),
            pltpu.VMEM((48, 128), F32),
            pltpu.VMEM((128, 640), BF16),
            pltpu.VMEM((4, PEERS, 48, 256), BF16),
            pltpu.VMEM((4, 48, 256 * PEERS), BF16),
            pltpu.VMEM((PEERS, 48, 128), BF16),
            pltpu.VMEM((4, 256 * PEERS, 256), BF16),
            pltpu.VMEM((NY, 48, 512), BF16),
            pltpu.VMEM((NY, 48, 512), BF16),
            pltpu.VMEM((8, 128), F32),
            pltpu.VMEM((NY, 8, 128), F32),
            pltpu.VMEM((2, 16, 256), BF16),
            pltpu.VMEM((2, 16, 256), BF16),
            pltpu.VMEM((2, 32, 128), BF16),
            pltpu.VMEM((2, 32, 128), BF16),
            dma,
            dma((7,)),
            dma((PEERS,)),
            dma((PEERS,)),
            dma((4, PEERS)),
            dma((4, PEERS)),
            dma((NY,)),
            dma((NY,)),
            dma((NY,)),
            dma((NY,)),
            dma((4,)),
            dma((4,)),
        ],
        compiler_params=pltpu.CompilerParams(
            collective_id=0, has_side_effects=True, vmem_limit_bytes=60 * 2**20
        ),
    )(
        frames, col_start, col_weights, footprint, jnp.transpose(row_start, (0, 2, 1)),
        jnp.transpose(row_weights, (0, 2, 3, 1)), seg_weight, feather_width,
    )


def solution(mesh):
    placed = (
        P("along", None, None, "across"),
        P("along", "across"),
        P("along", None, "across"),
        P("along", None),
        P("along", None, None),
        P("along", None, None, None),
        P("along", None),
        P("along", "across"),
    )
    return jax.shard_map(
        body, mesh=mesh, in_specs=placed, out_specs=P(None, "along", "across"), check_vma=False
    )
```

```python
import functools

import jax
import jax.numpy as jnp
from jax import lax
from jax.experimental import pallas as pl
from jax.experimental.pallas import tpu as pltpu
from jax.sharding import PartitionSpec as P

MESH = pl.DeviceIdType.MESH
F32 = jnp.float32
BF16 = jnp.bfloat16
NX, NY, NC = 4, 8, 2
PEERS = NX * NC
CHUNKS = ((5, 3), (4, 2), (6, 1), (7, 0))
GROUPS = ((0, 4), (1, 5), (3, 7), (2, 6))
PLACE = {r: 2 * g + i for g, group in enumerate(GROUPS) for i, r in enumerate(group)}


def taps(delta, weights):
    value = jnp.zeros(delta.shape, delta.dtype)
    for step, weight in enumerate(weights):
        value = jnp.where(delta == jnp.asarray(step, delta.dtype), weight, value)
    return value


def kernel(
    nz, frames, col_start, col_weights, footprint, row_start, row_weights, seg_weight, feather, out,
    image, starts_in, taps_in, places_in, rstart_in, rtaps_in, blend_in, width_in,
    table, places, blends, gather, lmat, outbox, inbox, params, cmat, ysend, yrecv, dsend, drecv, hsend, hrecv, ssend, srecv,
    load_sem, small_sem, px_s, px_r, x_s, x_r, y_s, y_r, d_s, d_r, h_s, h_r,
):
    a = lax.axis_index("along")
    z = lax.axis_index("across")
    x, y, c = a // (NY * NC), (a // NC) % NY, a % NC

    def along(xx, yy, cc):
        return ((xx % NX) * NY + (yy % NY)) * NC + cc

    def x_peer(r):
        return (along(x + r % NX, y, (c + r // NX) % NC), z)

    def y_peer(rel):
        return (along(x, y + rel, c), z)

    after, before = (a + 1) % 64, (a + 63) % 64
    extra = (a + 63 + 2 * c) % 64
    barrier = pltpu.get_barrier_semaphore()
    friends = [x_peer(r) for r in range(1, PEERS)] + [y_peer(r) for r in range(1, NY)] + [(extra, z)]
    if nz > 1:
        friends += [(a, (z + 1) % nz), (a, (z + nz - 1) % nz)]
    for friend in friends:
        pl.semaphore_signal(barrier, inc=1, device_id=friend, device_id_type=MESH)

    load = pltpu.make_async_copy(frames.at[0], image.at[:, pl.ds(0, 528), :], load_sem)
    load.start()
    small = [
        pltpu.make_async_copy(src, dst, small_sem.at[i])
        for i, (src, dst) in enumerate(
            (
                (footprint, places_in),
                (row_start.at[0], rstart_in),
                (row_weights.at[0], rtaps_in),
                (seg_weight, blend_in),
                (col_weights.at[0], taps_in),
                (col_start, starts_in),
                (feather, width_in),
            )
        )
    ]
    for copy in small:
        copy.start()
    image[:, 528:, :] = jnp.zeros((3, 112, 256), BF16)
    places[...] = jnp.full((8, 128), -1, jnp.int32)
    blends[...] = jnp.zeros((8, 128), F32)
    for copy in small:
        copy.wait()
    places[0:1, 0:33] = places_in[...]
    blends[0:1, 0:33] = blend_in[...].astype(F32)
    table[...] = jnp.zeros((128, 128), F32)
    table[0:8, 0:33] = rstart_in[...].astype(F32)
    for b in range(4):
        table[8 * (b + 1):8 * (b + 2), 0:33] = rtaps_in[b].astype(F32)

    row = lax.broadcasted_iota(jnp.int32, (128, 128), 0)
    lane = lax.broadcasted_iota(jnp.int32, (128, 128), 1)
    spread_row = lax.broadcasted_iota(jnp.int32, (128, 640), 0)
    spread_lane = lax.broadcasted_iota(jnp.int32, (128, 640), 1)
    spread = (spread_row // 8 == spread_lane // 128).astype(F32).astype(BF16)
    same = ((lane % 8) == (row % 8)).astype(F32)
    peer = row // 16
    group = (x + peer % NX) % NX
    core = (c + peer // NX) % NC
    first = (row // 8) % 2 == 0
    fp_row = places[0:1, :]
    start = places[0:1, 0:1]
    blend_row = blends[0:1, :]
    ones = jnp.ones((128, 128), BF16)
    rows_table = table[...].astype(BF16)
    by_tile = jnp.dot(
        blends[...].astype(BF16), (lane - start == row).astype(F32).astype(BF16), preferred_element_type=F32
    )
    col_taps = taps_in[...].astype(F32)
    col_first = starts_in[...].astype(F32)
    for j in range(8):
        for b in range(4):
            gather[b * 8 + j:b * 8 + j + 1, :] = col_taps[b:b + 1, j * 128:(j + 1) * 128]
        gather[32 + j:33 + j, :] = col_first[:, j * 128:(j + 1) * 128]
    gather[40:48, :] = by_tile
    position = lax.broadcasted_iota(jnp.int32, (256, 128), 0).astype(F32).astype(BF16)

    def make_matrix(r):
        for j in range(8):
            rows = [params[r, b * 8 + j:b * 8 + j + 1, :] for b in range(5)]
            value = taps(position - rows[4], rows[:4])
            cmat[j // 2, PLACE[r] * 256:(PLACE[r] + 1) * 256, (j % 2) * 128:(j % 2 + 1) * 128] = value

    def make_chunk(k):
        rel = jnp.where(first, CHUNKS[k][0], CHUNKS[k][1])
        tile = group * 16 + 2 * ((y + rel) % NY) + core
        hit = (tile == fp_row).astype(F32)
        picked = same * lax.dot_general(
            hit.astype(BF16), rows_table, (((1,), (1,)), ((), ())), preferred_element_type=F32
        )
        blend = jnp.dot((hit * blend_row).astype(BF16), ones, preferred_element_type=F32)
        wide = jnp.dot(picked.astype(BF16), spread, preferred_element_type=F32)
        base = (lane - 16 * (tile - start)).astype(F32) - wide[:, :128]
        weights = [wide[:, 128 * (b + 1):128 * (b + 2)] for b in range(4)]
        for part in range(5):
            lmat[:, part * 128:(part + 1) * 128] = taps(base + float(128 * part), weights).astype(BF16)
        blend = jnp.concatenate([blend, blend], axis=1)
        rows = [jnp.dot(lmat[...], image[ch], preferred_element_type=F32) * blend for ch in range(3)]
        for r in range(PEERS):
            block = jnp.concatenate(
                [rows[ch][r * 16 + m * 8:r * 16 + m * 8 + 8] for m in range(2) for ch in range(3)], axis=0
            ).astype(BF16)
            if r == 0:
                inbox[k, :, 0:256] = block
            else:
                outbox[k, r] = block

    def copy_params(r):
        return pltpu.make_async_remote_copy(
            src_ref=params.at[max(r - NX, 0)], dst_ref=params.at[r], send_sem=px_s.at[r], recv_sem=px_r.at[r],
            device_id=x_peer(min(r, NX)), device_id_type=MESH,
        )

    def copy_chunk(k, r):
        return pltpu.make_async_remote_copy(
            src_ref=outbox.at[k, r], dst_ref=inbox.at[k, :, pl.ds(PLACE[r] * 256, 256)],
            send_sem=x_s.at[k, r], recv_sem=x_r.at[k, r], device_id=x_peer(r), device_id_type=MESH,
        )

    def copy_sum(slot):
        hop = {1: 1, 2: 2, 3: 1, 4: 4, 5: 7, 6: 6, 7: 7}[slot]
        return pltpu.make_async_remote_copy(
            src_ref=ysend.at[slot], dst_ref=yrecv.at[slot],
            send_sem=y_s.at[slot], recv_sem=y_r.at[slot], device_id=y_peer(hop), device_id_type=MESH,
        )

    def copy_weight(rel):
        return pltpu.make_async_remote_copy(
            src_ref=dsend, dst_ref=drecv.at[rel], send_sem=d_s.at[rel], recv_sem=d_r.at[rel],
            device_id=y_peer(rel), device_id_type=MESH,
        )

    order = (2, 6, 1, 3, 5, 7, 4)
    params[0] = gather[...].astype(BF16)
    load.wait()
    make_chunk(0)
    pl.semaphore_wait(barrier, len(friends))
    for r in (2, 1, 3, 4):
        copy_params(r).start()
    for r in order:
        copy_chunk(0, r).start()
    make_chunk(1)
    for r in order:
        copy_chunk(1, r).start()
    make_chunk(2)
    for r in order:
        copy_chunk(2, r).start()
    make_chunk(3)
    for r in order:
        copy_chunk(3, r).start()
    make_matrix(0)
    weight = params[0, 32:48, :].astype(F32)
    for r in (4, 1, 3, 2, 5, 7, 6):
        copy_params(r).wait_recv()
        if r < NX:
            copy_params(r + NX).start()
        make_matrix(r)
        weight = weight + params[r, 32:48, :].astype(F32)
    weight = weight[8:16]
    dsend[...] = weight
    for rel in range(1, NY):
        copy_weight(rel).start()

    held = {}
    for k in range(4):
        total = [0.0] * 4
        for g, group in enumerate(GROUPS):
            for r in group:
                if r:
                    copy_chunk(k, r).wait_recv()
            left = inbox[k, :, g * 512:(g + 1) * 512]
            total = [
                total[n] + jnp.dot(left, cmat[n, g * 512:(g + 1) * 512], preferred_element_type=F32)
                for n in range(4)
            ]
        total = jnp.concatenate(total, axis=1)
        for m in range(2):
            rel = CHUNKS[k][m]
            part = total[m * 24:(m + 1) * 24]
            held[rel] = folded = jnp.concatenate([part[:, :512], part[:, 512:]], axis=0)
            if rel in (1, 3, 4, 5, 7):
                ysend[rel] = folded.astype(BF16)
                copy_sum(rel).start()
        if k == 2:
            for rel, near in ((2, 3), (6, 5)):
                copy_sum(near).wait_recv()
                ysend[rel] = (held[rel] + yrecv[near].astype(F32)).astype(BF16)
                copy_sum(rel).start()
    own = held[0]

    for rel in range(1, NY):
        copy_weight(rel).wait_recv()
        weight = weight + drecv[rel]
    here = lax.broadcasted_iota(jnp.int32, (8, 128), 1) == a
    divisor = jnp.sum(jnp.where(here, weight, 0.0), axis=1, keepdims=True)[0:1]
    for rel in (4, 2, 6, 1, 7):
        copy_sum(rel).wait_recv()
        own = own + yrecv[rel].astype(F32)
    own = own / divisor
    values = jnp.concatenate([own[:24], own[24:]], axis=1).astype(BF16).astype(F32)

    blank = jnp.zeros((1, 256), F32)

    def edge_rows(i):
        pieces = []
        for j in range(4):
            pieces += [values[ch * 8 + i:ch * 8 + i + 1, j * 256:(j + 1) * 256] for ch in range(3)] + [blank]
        return jnp.concatenate(pieces, axis=0).astype(BF16)

    pad = jnp.zeros((8, 128), F32)
    hsend[0] = edge_rows(7)
    hsend[1] = edge_rows(0)
    ssend[0] = jnp.concatenate([values[:, 896:], pad], axis=0).astype(BF16)
    ssend[1] = jnp.concatenate([values[:, :128], pad], axis=0).astype(BF16)
    halo = [
        pltpu.make_async_remote_copy(
            src_ref=hsend.at[side], dst_ref=hrecv.at[side], send_sem=h_s.at[side], recv_sem=h_r.at[side],
            device_id=(after if side == 0 else before, z), device_id_type=MESH,
        )
        for side in range(2)
    ]
    if nz > 1:
        halo += [
            pltpu.make_async_remote_copy(
                src_ref=ssend.at[side], dst_ref=srecv.at[side], send_sem=h_s.at[2 + side],
                recv_sem=h_r.at[2 + side],
                device_id=(a, (z + 1) % nz if side == 0 else (z + nz - 1) % nz), device_id_type=MESH,
            )
            for side in range(2)
        ]
    for copy in halo:
        copy.start()

    def opened(side):
        got = hrecv[side].astype(F32)
        return [
            jnp.concatenate([got[4 * j + ch:4 * j + ch + 1] for j in range(4)], axis=1) for ch in range(3)
        ]

    width = width_in[...].astype(F32)
    row8 = lax.broadcasted_iota(jnp.int32, (8, 1024), 0).astype(F32)
    col8 = lax.broadcasted_iota(jnp.int32, (8, 1024), 1).astype(F32)
    has_up = (a > 0).astype(F32)
    has_down = (a < 63).astype(F32)
    has_left = (z > 0).astype(F32)
    has_right = (z < nz - 1).astype(F32)
    top = 0.5 * jnp.maximum(0.0, 1.0 - row8 / width) * has_up
    bottom = 0.5 * jnp.maximum(0.0, 1.0 - (7.0 - row8) / width) * has_down
    ramp_left = 0.5 * jnp.maximum(0.0, 1.0 - col8 / width) * has_left
    ramp_right = 0.5 * jnp.maximum(0.0, 1.0 - (1023.0 - col8) / width) * has_right
    base = []
    for ch in range(3):
        tile = values[ch * 8:(ch + 1) * 8]
        result = tile - top * tile[0:1] - bottom * tile[7:8]
        if nz > 1:
            result = result - ramp_left * tile[:, 0:1] - ramp_right * tile[:, 1023:]
        base.append(result)
    for copy in halo:
        copy.wait_recv()
    up, down = opened(0), opened(1)
    for ch in range(3):
        result = base[ch] + top * up[ch] + bottom * down[ch]
        if nz > 1:
            left_col = srecv[0, ch * 8:(ch + 1) * 8, 127:128].astype(F32)
            right_col = srecv[1, ch * 8:(ch + 1) * 8, 0:1].astype(F32)
            result = result + ramp_left * left_col + ramp_right * right_col
        out[ch] = result.astype(BF16)

    for r in range(1, PEERS):
        copy_params(r).wait_send()
        for k in range(4):
            copy_chunk(k, r).wait_send()
    for rel in range(1, NY):
        copy_weight(rel).wait_send()
    for slot in range(1, NY):
        copy_sum(slot).wait_send()
    for copy in halo:
        copy.wait_send()


def body(
    frames, col_start, col_weights, footprint, row_start, row_weights, seg_weight, feather_width
):
    nz = lax.axis_size("across")
    held = [
        pltpu.with_memory_space_constraint(value, pltpu.HBM)
        for value in (
            frames, col_start, col_weights, footprint, jnp.transpose(row_start, (0, 2, 1)),
            jnp.transpose(row_weights, (0, 2, 3, 1)), seg_weight,
        )
    ]
    vmem = pl.BlockSpec(memory_space=pltpu.VMEM)
    dma = pltpu.SemaphoreType.DMA
    return pl.pallas_call(
        functools.partial(kernel, nz),
        out_shape=jax.ShapeDtypeStruct((3, 8, 1024), BF16),
        in_specs=[pl.BlockSpec(memory_space=pltpu.HBM)] * 8,
        out_specs=vmem,
        scratch_shapes=[
            pltpu.VMEM((3, 640, 256), BF16),
            pltpu.VMEM((1, 1024), jnp.int32),
            pltpu.VMEM((4, 1024), BF16),
            pltpu.VMEM((1, 33), jnp.int32),
            pltpu.VMEM((8, 33), jnp.int32),
            pltpu.VMEM((4, 8, 33), BF16),
            pltpu.VMEM((1, 33), BF16),
            pltpu.VMEM((1, 1), jnp.int32),
            pltpu.VMEM((128, 128), F32),
            pltpu.VMEM((8, 128), jnp.int32),
            pltpu.VMEM((8, 128), F32),
            pltpu.VMEM((48, 128), F32),
            pltpu.VMEM((128, 640), BF16),
            pltpu.VMEM((4, PEERS, 48, 256), BF16),
            pltpu.VMEM((4, 48, 256 * PEERS), BF16),
            pltpu.VMEM((PEERS, 48, 128), BF16),
            pltpu.VMEM((4, 256 * PEERS, 256), BF16),
            pltpu.VMEM((NY, 48, 512), BF16),
            pltpu.VMEM((NY, 48, 512), BF16),
            pltpu.VMEM((8, 128), F32),
            pltpu.VMEM((NY, 8, 128), F32),
            pltpu.VMEM((2, 16, 256), BF16),
            pltpu.VMEM((2, 16, 256), BF16),
            pltpu.VMEM((2, 32, 128), BF16),
            pltpu.VMEM((2, 32, 128), BF16),
            dma,
            dma((7,)),
            dma((PEERS,)),
            dma((PEERS,)),
            dma((4, PEERS)),
            dma((4, PEERS)),
            dma((NY,)),
            dma((NY,)),
            dma((NY,)),
            dma((NY,)),
            dma((4,)),
            dma((4,)),
        ],
        compiler_params=pltpu.CompilerParams(
            collective_id=0, has_side_effects=True, vmem_limit_bytes=48 * 2**20
        ),
    )(*held, feather_width)


def solution(mesh):
    placed = (
        P("along", None, None, "across"),
        P("along", "across"),
        P("along", None, "across"),
        P("along", None),
        P("along", None, None),
        P("along", None, None, None),
        P("along", None),
        P("along", "across"),
    )
    return jax.shard_map(
        body, mesh=mesh, in_specs=placed, out_specs=P(None, "along", "across"), check_vma=False
    )
```

```python
import functools

import jax
import jax.numpy as jnp
from jax import lax
from jax.experimental import pallas as pl
from jax.experimental.pallas import tpu as pltpu
from jax.sharding import PartitionSpec as P

MESH = pl.DeviceIdType.MESH
F32 = jnp.float32
BF16 = jnp.bfloat16
NX, NY, NC = 4, 8, 2
PEERS = NX * NC
CHUNKS = ((5, 3), (4, 2), (6, 0), (7, 1))
GROUPS = ((0, 4), (1, 5), (3, 7), (2, 6))
PLACE = {r: 2 * g + i for g, group in enumerate(GROUPS) for i, r in enumerate(group)}


def taps(delta, weights):
    value = jnp.zeros(delta.shape, delta.dtype)
    for step, weight in enumerate(weights):
        value = jnp.where(delta == jnp.asarray(step, delta.dtype), weight, value)
    return value


def kernel(
    nz, frames, col_start, col_weights, footprint, row_start, row_weights, seg_weight, feather, out,
    image, starts_in, taps_in, places_in, rstart_in, rtaps_in, blend_in, width_in,
    table, places, blends, gather, lmat, outbox, inbox, params, cmat, ysend, yrecv, dsend, drecv, hsend, hrecv, ssend, srecv,
    load_sem, small_sem, px_s, px_r, x_s, x_r, y_s, y_r, d_s, d_r, h_s, h_r,
):
    a = lax.axis_index("along")
    z = lax.axis_index("across")
    x, y, c = a // (NY * NC), (a // NC) % NY, a % NC

    def along(xx, yy, cc):
        return ((xx % NX) * NY + (yy % NY)) * NC + cc

    def x_peer(r):
        return (along(x + r % NX, y, (c + r // NX) % NC), z)

    def y_peer(rel):
        return (along(x, y + rel, c), z)

    after, before = (a + 1) % 64, (a + 63) % 64
    extra = (a + 63 + 2 * c) % 64
    barrier = pltpu.get_barrier_semaphore()
    friends = [x_peer(r) for r in range(1, PEERS)] + [y_peer(r) for r in range(1, NY)] + [(extra, z)]
    if nz > 1:
        friends += [(a, (z + 1) % nz), (a, (z + nz - 1) % nz)]
    for friend in friends:
        pl.semaphore_signal(barrier, inc=1, device_id=friend, device_id_type=MESH)

    load = pltpu.make_async_copy(frames.at[0], image.at[:, pl.ds(0, 528), :], load_sem)
    load.start()
    small = [
        pltpu.make_async_copy(src, dst, small_sem.at[i])
        for i, (src, dst) in enumerate(
            (
                (footprint, places_in),
                (row_start.at[0], rstart_in),
                (row_weights.at[0], rtaps_in),
                (seg_weight, blend_in),
                (col_weights.at[0], taps_in),
                (col_start, starts_in),
                (feather, width_in),
            )
        )
    ]
    for copy in small:
        copy.start()
    image[:, 528:, :] = jnp.zeros((3, 112, 256), BF16)
    places[...] = jnp.full((8, 128), -1, jnp.int32)
    blends[...] = jnp.zeros((8, 128), F32)
    for copy in small:
        copy.wait()
    places[0:1, 0:33] = places_in[...]
    blends[0:1, 0:33] = blend_in[...].astype(F32)
    table[...] = jnp.zeros((128, 128), F32)
    table[0:8, 0:33] = rstart_in[...].astype(F32)
    for b in range(4):
        table[8 * (b + 1):8 * (b + 2), 0:33] = rtaps_in[b].astype(F32)

    row = lax.broadcasted_iota(jnp.int32, (128, 128), 0)
    lane = lax.broadcasted_iota(jnp.int32, (128, 128), 1)
    spread_row = lax.broadcasted_iota(jnp.int32, (128, 640), 0)
    spread_lane = lax.broadcasted_iota(jnp.int32, (128, 640), 1)
    spread = (spread_row // 8 == spread_lane // 128).astype(F32).astype(BF16)
    same = ((lane % 8) == (row % 8)).astype(F32)
    peer = row // 16
    group = (x + peer % NX) % NX
    core = (c + peer // NX) % NC
    first = (row // 8) % 2 == 0
    fp_row = places[0:1, :]
    start = places[0:1, 0:1]
    blend_row = blends[0:1, :]
    ones = jnp.ones((128, 128), BF16)
    rows_table = table[...].astype(BF16)
    by_tile = jnp.dot(
        blends[...].astype(BF16), (lane - start == row).astype(F32).astype(BF16), preferred_element_type=F32
    )
    col_taps = taps_in[...].astype(F32)
    col_first = starts_in[...].astype(F32)
    for j in range(8):
        for b in range(4):
            gather[b * 8 + j:b * 8 + j + 1, :] = col_taps[b:b + 1, j * 128:(j + 1) * 128]
        gather[32 + j:33 + j, :] = col_first[:, j * 128:(j + 1) * 128]
    gather[40:48, :] = by_tile
    position = lax.broadcasted_iota(jnp.int32, (256, 128), 0).astype(F32).astype(BF16)

    def make_matrix(r):
        for j in range(8):
            rows = [params[r, b * 8 + j:b * 8 + j + 1, :] for b in range(5)]
            value = taps(position - rows[4], rows[:4])
            cmat[j // 2, PLACE[r] * 256:(PLACE[r] + 1) * 256, (j % 2) * 128:(j % 2 + 1) * 128] = value

    def make_chunk(k):
        rel = jnp.where(first, CHUNKS[k][0], CHUNKS[k][1])
        tile = group * 16 + 2 * ((y + rel) % NY) + core
        hit = (tile == fp_row).astype(F32)
        picked = same * lax.dot_general(
            hit.astype(BF16), rows_table, (((1,), (1,)), ((), ())), preferred_element_type=F32
        )
        blend = jnp.dot((hit * blend_row).astype(BF16), ones, preferred_element_type=F32)
        wide = jnp.dot(picked.astype(BF16), spread, preferred_element_type=F32)
        base = (lane - 16 * (tile - start)).astype(F32) - wide[:, :128]
        weights = [wide[:, 128 * (b + 1):128 * (b + 2)] for b in range(4)]
        for part in range(5):
            lmat[:, part * 128:(part + 1) * 128] = taps(base + float(128 * part), weights).astype(BF16)
        blend = jnp.concatenate([blend, blend], axis=1)
        rows = [jnp.dot(lmat[...], image[ch], preferred_element_type=F32) * blend for ch in range(3)]
        for r in range(PEERS):
            block = jnp.concatenate(
                [rows[ch][r * 16 + m * 8:r * 16 + m * 8 + 8] for m in range(2) for ch in range(3)], axis=0
            ).astype(BF16)
            if r == 0:
                inbox[k, :, 0:256] = block
            else:
                outbox[k, r] = block

    def copy_params(r):
        return pltpu.make_async_remote_copy(
            src_ref=params.at[max(r - NX, 0)], dst_ref=params.at[r], send_sem=px_s.at[r], recv_sem=px_r.at[r],
            device_id=x_peer(min(r, NX)), device_id_type=MESH,
        )

    def copy_chunk(k, r):
        return pltpu.make_async_remote_copy(
            src_ref=outbox.at[k, r], dst_ref=inbox.at[k, :, pl.ds(PLACE[r] * 256, 256)],
            send_sem=x_s.at[k, r], recv_sem=x_r.at[k, r], device_id=x_peer(r), device_id_type=MESH,
        )

    def copy_sum(slot):
        hop = {1: 1, 2: 2, 3: 1, 4: 4, 5: 7, 6: 6, 7: 7}[slot]
        return pltpu.make_async_remote_copy(
            src_ref=ysend.at[slot], dst_ref=yrecv.at[slot],
            send_sem=y_s.at[slot], recv_sem=y_r.at[slot], device_id=y_peer(hop), device_id_type=MESH,
        )

    def copy_weight(rel):
        return pltpu.make_async_remote_copy(
            src_ref=dsend, dst_ref=drecv.at[rel], send_sem=d_s.at[rel], recv_sem=d_r.at[rel],
            device_id=y_peer(rel), device_id_type=MESH,
        )

    order = (1, 2, 3, 5, 6, 7, 4)
    params[0] = gather[...].astype(BF16)
    load.wait()
    make_chunk(0)
    pl.semaphore_wait(barrier, len(friends))
    for r in (2, 1, 3, 4):
        copy_params(r).start()
    for r in order:
        copy_chunk(0, r).start()
    make_chunk(1)
    for r in order:
        copy_chunk(1, r).start()
    make_chunk(2)
    for r in order:
        copy_chunk(2, r).start()
    make_chunk(3)
    for r in order:
        copy_chunk(3, r).start()
    make_matrix(0)
    weight = params[0, 32:48, :].astype(F32)
    for r in (4, 1, 3, 2, 5, 7, 6):
        copy_params(r).wait_recv()
        if r < NX:
            copy_params(r + NX).start()
        make_matrix(r)
        weight = weight + params[r, 32:48, :].astype(F32)
    weight = weight[8:16]
    dsend[...] = weight
    for rel in range(1, NY):
        copy_weight(rel).start()

    held = {}
    for k in range(4):
        total = [0.0] * 4
        for g, group in enumerate(GROUPS):
            for r in group:
                if r:
                    copy_chunk(k, r).wait_recv()
            left = inbox[k, :, g * 512:(g + 1) * 512]
            total = [
                total[n] + jnp.dot(left, cmat[n, g * 512:(g + 1) * 512], preferred_element_type=F32)
                for n in range(4)
            ]
        total = jnp.concatenate(total, axis=1)
        for m in range(2):
            rel = CHUNKS[k][m]
            part = total[m * 24:(m + 1) * 24]
            held[rel] = folded = jnp.concatenate([part[:, :512], part[:, 512:]], axis=0)
            if rel in (1, 3, 4, 5, 7):
                ysend[rel] = folded.astype(BF16)
                copy_sum(rel).start()
        if k == 2:
            for rel, near in ((2, 3), (6, 5)):
                copy_sum(near).wait_recv()
                ysend[rel] = (held[rel] + yrecv[near].astype(F32)).astype(BF16)
                copy_sum(rel).start()
    own = held[0]

    for rel in range(1, NY):
        copy_weight(rel).wait_recv()
        weight = weight + drecv[rel]
    here = lax.broadcasted_iota(jnp.int32, (8, 128), 1) == a
    divisor = jnp.sum(jnp.where(here, weight, 0.0), axis=1, keepdims=True)[0:1]
    for rel in (4, 2, 6, 1, 7):
        copy_sum(rel).wait_recv()
        own = own + yrecv[rel].astype(F32)
    own = own / divisor
    values = jnp.concatenate([own[:24], own[24:]], axis=1).astype(BF16).astype(F32)

    blank = jnp.zeros((1, 256), F32)

    def edge_rows(i):
        pieces = []
        for j in range(4):
            pieces += [values[ch * 8 + i:ch * 8 + i + 1, j * 256:(j + 1) * 256] for ch in range(3)] + [blank]
        return jnp.concatenate(pieces, axis=0).astype(BF16)

    pad = jnp.zeros((8, 128), F32)
    hsend[0] = edge_rows(7)
    hsend[1] = edge_rows(0)
    ssend[0] = jnp.concatenate([values[:, 896:], pad], axis=0).astype(BF16)
    ssend[1] = jnp.concatenate([values[:, :128], pad], axis=0).astype(BF16)
    halo = [
        pltpu.make_async_remote_copy(
            src_ref=hsend.at[side], dst_ref=hrecv.at[side], send_sem=h_s.at[side], recv_sem=h_r.at[side],
            device_id=(after if side == 0 else before, z), device_id_type=MESH,
        )
        for side in range(2)
    ]
    if nz > 1:
        halo += [
            pltpu.make_async_remote_copy(
                src_ref=ssend.at[side], dst_ref=srecv.at[side], send_sem=h_s.at[2 + side],
                recv_sem=h_r.at[2 + side],
                device_id=(a, (z + 1) % nz if side == 0 else (z + nz - 1) % nz), device_id_type=MESH,
            )
            for side in range(2)
        ]
    for copy in halo:
        copy.start()

    def opened(side):
        got = hrecv[side].astype(F32)
        return [
            jnp.concatenate([got[4 * j + ch:4 * j + ch + 1] for j in range(4)], axis=1) for ch in range(3)
        ]

    width = width_in[...].astype(F32)
    row8 = lax.broadcasted_iota(jnp.int32, (8, 1024), 0).astype(F32)
    col8 = lax.broadcasted_iota(jnp.int32, (8, 1024), 1).astype(F32)
    has_up = (a > 0).astype(F32)
    has_down = (a < 63).astype(F32)
    has_left = (z > 0).astype(F32)
    has_right = (z < nz - 1).astype(F32)
    top = 0.5 * jnp.maximum(0.0, 1.0 - row8 / width) * has_up
    bottom = 0.5 * jnp.maximum(0.0, 1.0 - (7.0 - row8) / width) * has_down
    ramp_left = 0.5 * jnp.maximum(0.0, 1.0 - col8 / width) * has_left
    ramp_right = 0.5 * jnp.maximum(0.0, 1.0 - (1023.0 - col8) / width) * has_right
    base = []
    for ch in range(3):
        tile = values[ch * 8:(ch + 1) * 8]
        result = tile - top * tile[0:1] - bottom * tile[7:8]
        if nz > 1:
            result = result - ramp_left * tile[:, 0:1] - ramp_right * tile[:, 1023:]
        base.append(result)
    for copy in halo:
        copy.wait_recv()
    up, down = opened(0), opened(1)
    for ch in range(3):
        result = base[ch] + top * up[ch] + bottom * down[ch]
        if nz > 1:
            left_col = srecv[0, ch * 8:(ch + 1) * 8, 127:128].astype(F32)
            right_col = srecv[1, ch * 8:(ch + 1) * 8, 0:1].astype(F32)
            result = result + ramp_left * left_col + ramp_right * right_col
        out[ch] = result.astype(BF16)

    for r in range(1, PEERS):
        copy_params(r).wait_send()
        for k in range(4):
            copy_chunk(k, r).wait_send()
    for rel in range(1, NY):
        copy_weight(rel).wait_send()
    for slot in range(1, NY):
        copy_sum(slot).wait_send()
    for copy in halo:
        copy.wait_send()


def body(
    frames, col_start, col_weights, footprint, row_start, row_weights, seg_weight, feather_width
):
    nz = lax.axis_size("across")
    held = [
        pltpu.with_memory_space_constraint(value, pltpu.HBM)
        for value in (
            frames, col_start, col_weights, footprint, jnp.transpose(row_start, (0, 2, 1)),
            jnp.transpose(row_weights, (0, 2, 3, 1)), seg_weight,
        )
    ]
    vmem = pl.BlockSpec(memory_space=pltpu.VMEM)
    dma = pltpu.SemaphoreType.DMA
    return pl.pallas_call(
        functools.partial(kernel, nz),
        out_shape=jax.ShapeDtypeStruct((3, 8, 1024), BF16),
        in_specs=[pl.BlockSpec(memory_space=pltpu.HBM)] * 8,
        out_specs=vmem,
        scratch_shapes=[
            pltpu.VMEM((3, 640, 256), BF16),
            pltpu.VMEM((1, 1024), jnp.int32),
            pltpu.VMEM((4, 1024), BF16),
            pltpu.VMEM((1, 33), jnp.int32),
            pltpu.VMEM((8, 33), jnp.int32),
            pltpu.VMEM((4, 8, 33), BF16),
            pltpu.VMEM((1, 33), BF16),
            pltpu.VMEM((1, 1), jnp.int32),
            pltpu.VMEM((128, 128), F32),
            pltpu.VMEM((8, 128), jnp.int32),
            pltpu.VMEM((8, 128), F32),
            pltpu.VMEM((48, 128), F32),
            pltpu.VMEM((128, 640), BF16),
            pltpu.VMEM((4, PEERS, 48, 256), BF16),
            pltpu.VMEM((4, 48, 256 * PEERS), BF16),
            pltpu.VMEM((PEERS, 48, 128), BF16),
            pltpu.VMEM((4, 256 * PEERS, 256), BF16),
            pltpu.VMEM((NY, 48, 512), BF16),
            pltpu.VMEM((NY, 48, 512), BF16),
            pltpu.VMEM((8, 128), F32),
            pltpu.VMEM((NY, 8, 128), F32),
            pltpu.VMEM((2, 16, 256), BF16),
            pltpu.VMEM((2, 16, 256), BF16),
            pltpu.VMEM((2, 32, 128), BF16),
            pltpu.VMEM((2, 32, 128), BF16),
            dma,
            dma((7,)),
            dma((PEERS,)),
            dma((PEERS,)),
            dma((4, PEERS)),
            dma((4, PEERS)),
            dma((NY,)),
            dma((NY,)),
            dma((NY,)),
            dma((NY,)),
            dma((4,)),
            dma((4,)),
        ],
        compiler_params=pltpu.CompilerParams(
            collective_id=0, has_side_effects=True, vmem_limit_bytes=48 * 2**20
        ),
    )(*held, feather_width)


def solution(mesh):
    placed = (
        P("along", None, None, "across"),
        P("along", "across"),
        P("along", None, "across"),
        P("along", None),
        P("along", None, None),
        P("along", None, None, None),
        P("along", None),
        P("along", "across"),
    )
    return jax.shard_map(
        body, mesh=mesh, in_specs=placed, out_specs=P(None, "along", "across"), check_vma=False
    )
```

```python
import functools

import jax
import jax.numpy as jnp
from jax import lax
from jax.experimental import pallas as pl
from jax.experimental.pallas import tpu as pltpu
from jax.sharding import PartitionSpec as P

MESH = pl.DeviceIdType.MESH
F32 = jnp.float32
BF16 = jnp.bfloat16
NX, NY, NC = 4, 8, 2
PEERS = NX * NC
CHUNKS = ((5, 3), (4, 2), (6, 0), (7, 1))
GROUPS = ((0, 4), (1, 5), (3, 7), (2, 6))
PLACE = {r: 2 * g + i for g, group in enumerate(GROUPS) for i, r in enumerate(group)}


def taps(delta, weights):
    value = jnp.zeros(delta.shape, delta.dtype)
    for step, weight in enumerate(weights):
        value = jnp.where(delta == jnp.asarray(step, delta.dtype), weight, value)
    return value


def kernel(
    nz, frames, col_start, col_weights, footprint, row_start, row_weights, seg_weight, feather, out,
    image, starts_in, taps_in, places_in, rstart_in, rtaps_in, blend_in, width_in,
    table, places, blends, gather, lmat, outbox, inbox, params, cmat, ysend, yrecv, dsend, drecv, hsend, hrecv, ssend, srecv,
    load_sem, small_sem, px_s, px_r, x_s, x_r, y_s, y_r, d_s, d_r, h_s, h_r,
):
    a = lax.axis_index("along")
    z = lax.axis_index("across")
    x, y, c = a // (NY * NC), (a // NC) % NY, a % NC

    def along(xx, yy, cc):
        return ((xx % NX) * NY + (yy % NY)) * NC + cc

    def x_peer(r):
        return (along(x + r % NX, y, (c + r // NX) % NC), z)

    def y_peer(rel):
        return (along(x, y + rel, c), z)

    after, before = (a + 1) % 64, (a + 63) % 64
    extra = (a + 63 + 2 * c) % 64
    barrier = pltpu.get_barrier_semaphore()
    friends = [x_peer(r) for r in range(1, PEERS)] + [y_peer(r) for r in range(1, NY)] + [(extra, z)]
    if nz > 1:
        friends += [(a, (z + 1) % nz), (a, (z + nz - 1) % nz)]
    for friend in friends:
        pl.semaphore_signal(barrier, inc=1, device_id=friend, device_id_type=MESH)

    load = pltpu.make_async_copy(frames.at[0], image.at[:, pl.ds(0, 528), :], load_sem)
    load.start()
    small = [
        pltpu.make_async_copy(src, dst, small_sem.at[i])
        for i, (src, dst) in enumerate(
            (
                (footprint, places_in),
                (row_start.at[0], rstart_in),
                (row_weights.at[0], rtaps_in),
                (seg_weight, blend_in),
                (col_weights.at[0], taps_in),
                (col_start, starts_in),
                (feather, width_in),
            )
        )
    ]
    for copy in small:
        copy.start()
    image[:, 528:, :] = jnp.zeros((3, 112, 256), BF16)
    places[...] = jnp.full((8, 128), -1, jnp.int32)
    blends[...] = jnp.zeros((8, 128), F32)
    for copy in small:
        copy.wait()
    places[0:1, 0:33] = places_in[...]
    blends[0:1, 0:33] = blend_in[...].astype(F32)
    table[...] = jnp.zeros((128, 128), F32)
    table[0:8, 0:33] = rstart_in[...].astype(F32)
    for b in range(4):
        table[8 * (b + 1):8 * (b + 2), 0:33] = rtaps_in[b].astype(F32)

    row = lax.broadcasted_iota(jnp.int32, (128, 128), 0)
    lane = lax.broadcasted_iota(jnp.int32, (128, 128), 1)
    spread_row = lax.broadcasted_iota(jnp.int32, (128, 640), 0)
    spread_lane = lax.broadcasted_iota(jnp.int32, (128, 640), 1)
    spread = (spread_row // 8 == spread_lane // 128).astype(F32).astype(BF16)
    same = ((lane % 8) == (row % 8)).astype(F32)
    peer = row // 16
    group = (x + peer % NX) % NX
    core = (c + peer // NX) % NC
    first = (row // 8) % 2 == 0
    fp_row = places[0:1, :]
    start = places[0:1, 0:1]
    blend_row = blends[0:1, :]
    ones = jnp.ones((128, 128), BF16)
    rows_table = table[...].astype(BF16)
    by_tile = jnp.dot(
        blends[...].astype(BF16), (lane - start == row).astype(F32).astype(BF16), preferred_element_type=F32
    )
    col_taps = taps_in[...].astype(F32)
    col_first = starts_in[...].astype(F32)
    for j in range(8):
        for b in range(4):
            gather[b * 8 + j:b * 8 + j + 1, :] = col_taps[b:b + 1, j * 128:(j + 1) * 128]
        gather[32 + j:33 + j, :] = col_first[:, j * 128:(j + 1) * 128]
    gather[40:48, :] = by_tile
    position = lax.broadcasted_iota(jnp.int32, (256, 128), 0).astype(F32).astype(BF16)

    def make_matrix(r):
        for j in range(8):
            rows = [params[r, b * 8 + j:b * 8 + j + 1, :] for b in range(5)]
            value = taps(position - rows[4], rows[:4])
            cmat[j // 2, PLACE[r] * 256:(PLACE[r] + 1) * 256, (j % 2) * 128:(j % 2 + 1) * 128] = value

    def make_chunk(k):
        rel = jnp.where(first, CHUNKS[k][0], CHUNKS[k][1])
        tile = group * 16 + 2 * ((y + rel) % NY) + core
        hit = (tile == fp_row).astype(F32)
        picked = same * lax.dot_general(
            hit.astype(BF16), rows_table, (((1,), (1,)), ((), ())), preferred_element_type=F32
        )
        blend = jnp.dot((hit * blend_row).astype(BF16), ones, preferred_element_type=F32)
        wide = jnp.dot(picked.astype(BF16), spread, preferred_element_type=F32)
        base = (lane - 16 * (tile - start)).astype(F32) - wide[:, :128]
        weights = [wide[:, 128 * (b + 1):128 * (b + 2)] for b in range(4)]
        for part in range(5):
            lmat[:, part * 128:(part + 1) * 128] = taps(base + float(128 * part), weights).astype(BF16)
        blend = jnp.concatenate([blend, blend], axis=1)
        rows = [jnp.dot(lmat[...], image[ch], preferred_element_type=F32) * blend for ch in range(3)]
        for r in range(PEERS):
            block = jnp.concatenate(
                [rows[ch][r * 16 + m * 8:r * 16 + m * 8 + 8] for m in range(2) for ch in range(3)], axis=0
            ).astype(BF16)
            if r == 0:
                inbox[k, :, 0:256] = block
            else:
                outbox[k, r] = block

    def copy_params(r):
        return pltpu.make_async_remote_copy(
            src_ref=params.at[max(r - NX, 0)], dst_ref=params.at[r], send_sem=px_s.at[r], recv_sem=px_r.at[r],
            device_id=x_peer(min(r, NX)), device_id_type=MESH,
        )

    def copy_chunk(k, r):
        return pltpu.make_async_remote_copy(
            src_ref=outbox.at[k, r], dst_ref=inbox.at[k, :, pl.ds(PLACE[r] * 256, 256)],
            send_sem=x_s.at[k, r], recv_sem=x_r.at[k, r], device_id=x_peer(r), device_id_type=MESH,
        )

    def copy_sum(slot):
        hop = {1: 1, 2: 2, 3: 1, 4: 4, 5: 7, 6: 6, 7: 7}[slot]
        return pltpu.make_async_remote_copy(
            src_ref=ysend.at[slot], dst_ref=yrecv.at[slot],
            send_sem=y_s.at[slot], recv_sem=y_r.at[slot], device_id=y_peer(hop), device_id_type=MESH,
        )

    def copy_weight(rel):
        return pltpu.make_async_remote_copy(
            src_ref=dsend, dst_ref=drecv.at[rel], send_sem=d_s.at[rel], recv_sem=d_r.at[rel],
            device_id=y_peer(rel), device_id_type=MESH,
        )

    order = (5, 6, 7, 1, 2, 3, 4)
    params[0] = gather[...].astype(BF16)
    load.wait()
    make_chunk(0)
    pl.semaphore_wait(barrier, len(friends))
    for r in (2, 1, 3, 4):
        copy_params(r).start()
    for r in order:
        copy_chunk(0, r).start()
    make_chunk(1)
    for r in order:
        copy_chunk(1, r).start()
    make_chunk(2)
    for r in order:
        copy_chunk(2, r).start()
    make_chunk(3)
    for r in order:
        copy_chunk(3, r).start()
    make_matrix(0)
    weight = params[0, 32:48, :].astype(F32)
    for r in (4, 1, 3, 2, 5, 7, 6):
        copy_params(r).wait_recv()
        if r < NX:
            copy_params(r + NX).start()
        make_matrix(r)
        weight = weight + params[r, 32:48, :].astype(F32)
    weight = weight[8:16]
    dsend[...] = weight
    for rel in range(1, NY):
        copy_weight(rel).start()

    held = {}
    for k in range(4):
        total = [0.0] * 4
        for g, group in enumerate(GROUPS):
            for r in group:
                if r:
                    copy_chunk(k, r).wait_recv()
            left = inbox[k, :, g * 512:(g + 1) * 512]
            total = [
                total[n] + jnp.dot(left, cmat[n, g * 512:(g + 1) * 512], preferred_element_type=F32)
                for n in range(4)
            ]
        total = jnp.concatenate(total, axis=1)
        for m in range(2):
            rel = CHUNKS[k][m]
            part = total[m * 24:(m + 1) * 24]
            held[rel] = folded = jnp.concatenate([part[:, :512], part[:, 512:]], axis=0)
            if rel in (1, 3, 4, 5, 7):
                ysend[rel] = folded.astype(BF16)
                copy_sum(rel).start()
        if k == 2:
            for rel, near in ((2, 3), (6, 5)):
                copy_sum(near).wait_recv()
                ysend[rel] = (held[rel] + yrecv[near].astype(F32)).astype(BF16)
                copy_sum(rel).start()
    own = held[0]

    for rel in range(1, NY):
        copy_weight(rel).wait_recv()
        weight = weight + drecv[rel]
    here = lax.broadcasted_iota(jnp.int32, (8, 128), 1) == a
    divisor = jnp.sum(jnp.where(here, weight, 0.0), axis=1, keepdims=True)[0:1]
    for rel in (4, 2, 6, 1, 7):
        copy_sum(rel).wait_recv()
        own = own + yrecv[rel].astype(F32)
    own = own / divisor
    values = jnp.concatenate([own[:24], own[24:]], axis=1).astype(BF16).astype(F32)

    blank = jnp.zeros((1, 256), F32)

    def edge_rows(i):
        pieces = []
        for j in range(4):
            pieces += [values[ch * 8 + i:ch * 8 + i + 1, j * 256:(j + 1) * 256] for ch in range(3)] + [blank]
        return jnp.concatenate(pieces, axis=0).astype(BF16)

    pad = jnp.zeros((8, 128), F32)
    hsend[0] = edge_rows(7)
    hsend[1] = edge_rows(0)
    ssend[0] = jnp.concatenate([values[:, 896:], pad], axis=0).astype(BF16)
    ssend[1] = jnp.concatenate([values[:, :128], pad], axis=0).astype(BF16)
    halo = [
        pltpu.make_async_remote_copy(
            src_ref=hsend.at[side], dst_ref=hrecv.at[side], send_sem=h_s.at[side], recv_sem=h_r.at[side],
            device_id=(after if side == 0 else before, z), device_id_type=MESH,
        )
        for side in range(2)
    ]
    if nz > 1:
        halo += [
            pltpu.make_async_remote_copy(
                src_ref=ssend.at[side], dst_ref=srecv.at[side], send_sem=h_s.at[2 + side],
                recv_sem=h_r.at[2 + side],
                device_id=(a, (z + 1) % nz if side == 0 else (z + nz - 1) % nz), device_id_type=MESH,
            )
            for side in range(2)
        ]
    for copy in halo:
        copy.start()

    def opened(side):
        got = hrecv[side].astype(F32)
        return [
            jnp.concatenate([got[4 * j + ch:4 * j + ch + 1] for j in range(4)], axis=1) for ch in range(3)
        ]

    width = width_in[...].astype(F32)
    row8 = lax.broadcasted_iota(jnp.int32, (8, 1024), 0).astype(F32)
    col8 = lax.broadcasted_iota(jnp.int32, (8, 1024), 1).astype(F32)
    has_up = (a > 0).astype(F32)
    has_down = (a < 63).astype(F32)
    has_left = (z > 0).astype(F32)
    has_right = (z < nz - 1).astype(F32)
    top = 0.5 * jnp.maximum(0.0, 1.0 - row8 / width) * has_up
    bottom = 0.5 * jnp.maximum(0.0, 1.0 - (7.0 - row8) / width) * has_down
    ramp_left = 0.5 * jnp.maximum(0.0, 1.0 - col8 / width) * has_left
    ramp_right = 0.5 * jnp.maximum(0.0, 1.0 - (1023.0 - col8) / width) * has_right
    base = []
    for ch in range(3):
        tile = values[ch * 8:(ch + 1) * 8]
        result = tile - top * tile[0:1] - bottom * tile[7:8]
        if nz > 1:
            result = result - ramp_left * tile[:, 0:1] - ramp_right * tile[:, 1023:]
        base.append(result)
    for copy in halo:
        copy.wait_recv()
    up, down = opened(0), opened(1)
    for ch in range(3):
        result = base[ch] + top * up[ch] + bottom * down[ch]
        if nz > 1:
            left_col = srecv[0, ch * 8:(ch + 1) * 8, 127:128].astype(F32)
            right_col = srecv[1, ch * 8:(ch + 1) * 8, 0:1].astype(F32)
            result = result + ramp_left * left_col + ramp_right * right_col
        out[ch] = result.astype(BF16)

    for r in range(1, PEERS):
        copy_params(r).wait_send()
        for k in range(4):
            copy_chunk(k, r).wait_send()
    for rel in range(1, NY):
        copy_weight(rel).wait_send()
    for slot in range(1, NY):
        copy_sum(slot).wait_send()
    for copy in halo:
        copy.wait_send()


def body(
    frames, col_start, col_weights, footprint, row_start, row_weights, seg_weight, feather_width
):
    nz = lax.axis_size("across")
    held = [
        pltpu.with_memory_space_constraint(value, pltpu.HBM)
        for value in (
            frames, col_start, col_weights, footprint, jnp.transpose(row_start, (0, 2, 1)),
            jnp.transpose(row_weights, (0, 2, 3, 1)), seg_weight,
        )
    ]
    vmem = pl.BlockSpec(memory_space=pltpu.VMEM)
    dma = pltpu.SemaphoreType.DMA
    return pl.pallas_call(
        functools.partial(kernel, nz),
        out_shape=jax.ShapeDtypeStruct((3, 8, 1024), BF16),
        in_specs=[pl.BlockSpec(memory_space=pltpu.HBM)] * 8,
        out_specs=vmem,
        scratch_shapes=[
            pltpu.VMEM((3, 640, 256), BF16),
            pltpu.VMEM((1, 1024), jnp.int32),
            pltpu.VMEM((4, 1024), BF16),
            pltpu.VMEM((1, 33), jnp.int32),
            pltpu.VMEM((8, 33), jnp.int32),
            pltpu.VMEM((4, 8, 33), BF16),
            pltpu.VMEM((1, 33), BF16),
            pltpu.VMEM((1, 1), jnp.int32),
            pltpu.VMEM((128, 128), F32),
            pltpu.VMEM((8, 128), jnp.int32),
            pltpu.VMEM((8, 128), F32),
            pltpu.VMEM((48, 128), F32),
            pltpu.VMEM((128, 640), BF16),
            pltpu.VMEM((4, PEERS, 48, 256), BF16),
            pltpu.VMEM((4, 48, 256 * PEERS), BF16),
            pltpu.VMEM((PEERS, 48, 128), BF16),
            pltpu.VMEM((4, 256 * PEERS, 256), BF16),
            pltpu.VMEM((NY, 48, 512), BF16),
            pltpu.VMEM((NY, 48, 512), BF16),
            pltpu.VMEM((8, 128), F32),
            pltpu.VMEM((NY, 8, 128), F32),
            pltpu.VMEM((2, 16, 256), BF16),
            pltpu.VMEM((2, 16, 256), BF16),
            pltpu.VMEM((2, 32, 128), BF16),
            pltpu.VMEM((2, 32, 128), BF16),
            dma,
            dma((7,)),
            dma((PEERS,)),
            dma((PEERS,)),
            dma((4, PEERS)),
            dma((4, PEERS)),
            dma((NY,)),
            dma((NY,)),
            dma((NY,)),
            dma((NY,)),
            dma((4,)),
            dma((4,)),
        ],
        compiler_params=pltpu.CompilerParams(
            collective_id=0, has_side_effects=True, vmem_limit_bytes=48 * 2**20
        ),
    )(*held, feather_width)


def solution(mesh):
    placed = (
        P("along", None, None, "across"),
        P("along", "across"),
        P("along", None, "across"),
        P("along", None),
        P("along", None, None),
        P("along", None, None, None),
        P("along", None),
        P("along", "across"),
    )
    return jax.shard_map(
        body, mesh=mesh, in_specs=placed, out_specs=P(None, "along", "across"), check_vma=False
    )
```
